512 devices in a mesh: ab: 4 (over x), ij: 16 (over y, core), cd: 8 (over z).
Axes of the slice: x: 4, y: 8, z: 8, core: 2. Of those that a mesh axis runs over, the one named last changes fastest.
Arguments:
- integrals: bfloat16 [1536, 163840], P('ab', ('cd', 'ij')), may hold values from -0.015625 to 0.015625
- amplitudes: bfloat16 [163840, 2048], P(('cd', 'ij'), 'ab'), may hold values from -24 to 24
Outputs:
- ladder: bfloat16 [1536, 2048], P(('ab', 'cd'), 'ij')
The draws below stay inside these ranges and needn't reach their ends.
All inputs are finite; a program needn't handle non-finite values.
Results may differ from the reference program's by a relative error of at most 0.0012.
Values may be sent and summed in bfloat16 or wider, within the bound.
A program may use at most 64 MiB of HBM per device.

```python
import jax
import jax.numpy as jnp
from jax import lax

CD = 163840
IJ = 2048
AB = 1536


def spiked(array, key, source, target, shards_of, factor):
    owner, partner = [(jnp.arange(array.shape[axis_at]) // (array.shape[axis_at] // shards_of)).reshape([-1 if axis == axis_at else 1 for axis in range(array.ndim)]) for axis_at in (source, target)]
    chosen = jax.random.permutation(key, shards_of)[partner]
    strong = (owner == chosen) | (owner == (partner + shards_of // 2) % shards_of)
    return jnp.where(strong, factor * array, array)


def shard_levels(key, dims, split, low, high):
    def one(axis_at, parts):
        draws = jax.random.uniform(jax.random.fold_in(jax.random.fold_in(key, 6), axis_at), (parts,), jnp.float32, low / len(split), high / len(split))
        return jnp.repeat(jnp.exp(draws), dims[axis_at] // parts).reshape((-1,) + (1,) * (len(dims) - axis_at - 1))

    factor_of = one(*split[0])
    for cut in split[1:]:
        factor_of = factor_of * one(*cut)
    return factor_of


def normal_values(rng, shape, width, bound, cuts=(), kind=jnp.bfloat16):
    loudness = shard_levels(rng, shape, cuts, -0.22, 0.18) if cuts else 1.0
    entries = jax.random.normal(rng, shape, jnp.float32) * width * loudness
    return jnp.minimum(jnp.maximum(entries, -bound), bound).astype(kind)


def heavy_noise(key, extent, scale, reach, pieces, heavy, kind=jnp.bfloat16):
    drawn = scale * jax.random.normal(key, extent, jnp.float32)
    if pieces:
        drawn = drawn * shard_levels(key, extent, pieces, -0.22, 0.18)
    return jnp.clip(spiked(drawn, jax.random.fold_in(key, 3), *heavy), -reach, reach).astype(kind)


def setup_inputs(seed: int = 0) -> dict:
    splits = jax.random.split(jax.random.key(seed), 3)
    integrals = normal_values(splits[0], (AB, CD), CD ** -0.5, 0.015625, ((0, 4), (1, 128)))
    amplitudes = heavy_noise(splits[1], (CD, IJ), 1.0, 24.0, ((0, 128), (1, 4)), (0, 1, 128, 5.5))
    return {"integrals": integrals, "amplitudes": amplitudes}


def reference(integrals, amplitudes):
    block = 8192
    count = integrals.shape[1] // block
    rest = integrals.shape[1] - count * block

    def add_block(total, index):
        start = (index * block).astype(jnp.int32)
        left = lax.dynamic_slice_in_dim(integrals, start, block, 1).astype(jnp.float32)
        right = lax.dynamic_slice_in_dim(amplitudes, start, block, 0).astype(jnp.float32)
        return total + jnp.dot(left, right, preferred_element_type=jnp.float32), None

    total = jnp.zeros((integrals.shape[0], amplitudes.shape[1]), jnp.float32)
    if count > 0:
        total, unused = lax.scan(add_block, total, jnp.arange(count, dtype=jnp.int32))
    if rest > 0:
        left = integrals[:, count * block:].astype(jnp.float32)
        right = amplitudes[count * block:, :].astype(jnp.float32)
        total = total + jnp.dot(left, right, preferred_element_type=jnp.float32)
    return total.astype(jnp.bfloat16)
```

```python
import jax
import jax.numpy as jnp
from jax import lax
from jax.experimental import pallas as pl
from jax.experimental.pallas import tpu as pltpu
from jax.sharding import PartitionSpec as P

MESH = pl.DeviceIdType.MESH
F32 = jnp.float32
BF16 = jnp.bfloat16
ROWS, DEPTH, COLS = 384, 1280, 512
N = 8
G = 48
W = 128


def kernel(v_hbm, t_hbm, out, v, t, p, sib, held, s1, r1, s2, fin,
           load_sem, xs_sem, xr_sem, cs_sem, cr_sem, s1s_sem, s1r_sem, s2s_sem, s2r_sem, fs_sem, fr_sem):
    x, ij, z = lax.axis_index("ab"), lax.axis_index("ij"), lax.axis_index("cd")
    y, c = ij // 2, ij % 2
    xv, xt = x + 1 - 2 * (x % 2), 3 - x
    me1 = z + c * (y - z)
    me2 = y + c * (z - y)

    def at(xx, ii, zz):
        return {"ab": xx, "ij": ii, "cd": zz}

    def first(q):
        return at(x, 2 * (y + c * (q - y)) + c, z + (1 - c) * (q - z))

    def second(q):
        return at(x, 2 * (y + (1 - c) * (q - y)) + c, z + c * (q - z))

    twin = at(x, ij + 1 - 2 * c, z)

    s_mine = me2 // 4
    j_mine = 2 * (me2 % 4) + c + s_mine * (1 - 2 * c)
    owner_x = x + s_mine * (xv - x)
    owner_ij = 4 * (x + (j_mine // 4) * (xt - x)) + j_mine % 4
    owner_is_me = (owner_x == x) & (owner_ij == ij) & (me1 == z)

    slab = ij // 4
    near = (slab == x) | (slab == 3 - x)
    src_s = jnp.where(near, 0, 1)
    src_x = x + src_s * (xv - x)
    src_j = jnp.where(slab == src_x, 0, 4) + ij % 4
    src_c = (src_s + src_j) % 2
    src_q = 4 * src_s + src_j // 2
    src_y = src_q + src_c * (z - src_q)
    src_z = z + src_c * (src_q - z)
    src_ij = 2 * src_y + src_c

    barrier = pltpu.get_barrier_semaphore()

    def greet(device):
        pl.semaphore_signal(barrier, inc=1, device_id=device, device_id_type=MESH)

    greet(at(xv, ij, z))
    greet(at(xt, ij, z))
    greet(twin)
    for d in range(1, N):
        greet(first((me1 + d) % N))
        greet(second((me2 + d) % N))

    @pl.when(jnp.logical_not(owner_is_me))
    def _():
        greet(at(owner_x, owner_ij, me1))
        greet(at(src_x, src_ij, src_z))

    load_v = pltpu.make_async_copy(v_hbm, v.at[0], load_sem.at[0])
    load_t = pltpu.make_async_copy(t_hbm, t.at[:, pl.ds(0, COLS)], load_sem.at[1])
    load_v.start()
    load_t.start()

    @pl.when(jnp.logical_not(owner_is_me))
    def _():
        pl.semaphore_wait(barrier, 5 + 2 * (N - 1))

    @pl.when(owner_is_me)
    def _():
        pl.semaphore_wait(barrier, 3 + 2 * (N - 1))

    swaps = []
    for i in range(4):
        swaps.append(pltpu.make_async_remote_copy(
            src_ref=t_hbm.at[:, pl.ds(i * W, W)], dst_ref=t.at[:, pl.ds(COLS + i * W, W)],
            send_sem=xs_sem.at[i], recv_sem=xr_sem.at[i], device_id=at(xt, ij, z), device_id_type=MESH))
    swaps.append(pltpu.make_async_remote_copy(
        src_ref=v_hbm, dst_ref=v.at[1], send_sem=xs_sem.at[4], recv_sem=xr_sem.at[4],
        device_id=at(xv, ij, z), device_id_type=MESH))
    for i in (0, 4, 1, 2, 3):
        swaps[i].start()

    def half(q):
        s = q // 4
        return c + s * (1 - 2 * c)

    def to_twin(q):
        pltpu.make_async_remote_copy(
            src_ref=p.at[q, 1 - half(q)], dst_ref=sib.at[q], send_sem=cs_sem, recv_sem=cr_sem.at[q],
            device_id=twin, device_id_type=MESH).start()

    def pair(q):
        res = jnp.dot(v[q // 4], t[:, pl.ds(256 * (q % 4), 256)], preferred_element_type=F32)
        p[q, 0] = res[:, :W]
        p[q, 1] = res[:, W:]
        to_twin(q)

    def single(s, j):
        q = 4 * s + j // 2
        p[q, j % 2] = jnp.dot(v[s], t[:, pl.ds(W * j, W)], preferred_element_type=F32)

        @pl.when(c != (s + j) % 2)
        def _():
            to_twin(q)

    def scatter(q):
        pltpu.make_async_copy(sib.at[q], sib.at[q], cr_sem.at[q]).wait()
        held[q] = p[q, half(q)] + sib[q]
        for d in range(1, N):
            to = (me1 + d) % N
            pltpu.make_async_remote_copy(
                src_ref=held.at[q, pl.ds(pl.multiple_of(to * G, G), G)], dst_ref=s1.at[q, d],
                send_sem=s1s_sem, recv_sem=s1r_sem.at[q], device_id=first(to), device_id_type=MESH).start()

    def gather(q):
        pltpu.make_async_copy(s1.at[q, pl.ds(1, N - 1)], s1.at[q, pl.ds(1, N - 1)], s1r_sem.at[q]).wait()
        total = held[q, pl.ds(pl.multiple_of(me1 * G, G), G), :]
        for d in range(1, N):
            total = total + s1[q, d]
        r1[q] = total
        d = (q - me2 + N) % N

        @pl.when(d == 0)
        def _():
            s2[0] = total

        @pl.when(d != 0)
        def _():
            pltpu.make_async_remote_copy(
                src_ref=r1.at[q], dst_ref=s2.at[d], send_sem=s2s_sem, recv_sem=s2r_sem,
                device_id=second(q), device_id_type=MESH).start()

    load_v.wait()
    load_t.wait()
    pair(0)
    pair(1)
    scatter(0)
    scatter(1)
    swaps[0].wait_recv()
    single(0, 4)
    swaps[1].wait_recv()
    single(0, 5)
    scatter(2)
    swaps[4].wait_recv()
    pair(4)
    pair(5)
    scatter(4)
    single(1, 4)
    single(1, 5)
    scatter(5)
    scatter(6)
    gather(0)
    gather(1)
    gather(2)
    swaps[2].wait_recv()
    single(0, 6)
    single(1, 6)
    scatter(3 + 4 * c)
    gather(4)
    gather(5)
    gather(6)
    gather(3 + 4 * c)
    swaps[3].wait_recv()
    single(0, 7)
    single(1, 7)
    scatter(7 - 4 * c)
    gather(7 - 4 * c)

    pltpu.make_async_copy(s2.at[pl.ds(1, N - 1)], s2.at[pl.ds(1, N - 1)], s2r_sem).wait()
    total = s2[0]
    for d in range(1, N):
        total = total + s2[d]
    fin[...] = total.astype(BF16)

    @pl.when(owner_is_me)
    def _():
        out[...] = fin[...]

    @pl.when(jnp.logical_not(owner_is_me))
    def _():
        last = pltpu.make_async_remote_copy(
            src_ref=fin, dst_ref=out, send_sem=fs_sem, recv_sem=fr_sem,
            device_id=at(owner_x, owner_ij, me1), device_id_type=MESH)
        last.start()
        last.wait()

    for swap in swaps:
        swap.wait_send()
    pltpu.make_async_copy(sib, sib, cs_sem).wait()
    pltpu.make_async_copy(s1.at[:, pl.ds(1, N - 1)], s1.at[:, pl.ds(1, N - 1)], s1s_sem).wait()
    pltpu.make_async_copy(s2.at[pl.ds(1, N - 1)], s2.at[pl.ds(1, N - 1)], s2s_sem).wait()


def per_device(integrals, amplitudes):
    dma, vmem = pltpu.SemaphoreType.DMA, pltpu.VMEM
    return pl.pallas_call(
        kernel,
        out_shape=jax.ShapeDtypeStruct((G, W), BF16),
        in_specs=[pl.BlockSpec(memory_space=pl.ANY)] * 2,
        out_specs=pl.BlockSpec(memory_space=pltpu.VMEM),
        scratch_shapes=[
            vmem((2, ROWS, DEPTH), BF16),
            vmem((DEPTH, 2 * COLS), BF16),
            vmem((N, 2, ROWS, W), F32),
            vmem((N, ROWS, W), F32),
            vmem((N, ROWS, W), F32),
            vmem((N, N, G, W), F32),
            vmem((N, G, W), F32),
            vmem((N, G, W), F32),
            vmem((G, W), BF16),
            dma((2,)), dma((5,)), dma((5,)),
            dma, dma((N,)), dma, dma((N,)), dma, dma, dma, dma,
        ],
        compiler_params=pltpu.CompilerParams(
            collective_id=0, has_side_effects=True, vmem_limit_bytes=48 << 20
        ),
    )(integrals, amplitudes)


def solution(mesh):
    placed = (P("ab", ("cd", "ij")), P(("cd", "ij"), "ab"))
    return jax.shard_map(
        per_device, mesh=mesh, in_specs=placed, out_specs=P(("ab", "cd"), "ij"), check_vma=False
    )
```

```python
import jax
import jax.numpy as jnp
from jax import lax
from jax.experimental import pallas as pl
from jax.experimental.pallas import tpu as pltpu
from jax.sharding import PartitionSpec as P

MESH = pl.DeviceIdType.MESH
F32 = jnp.float32
BF16 = jnp.bfloat16
ROWS, DEPTH, COLS = 384, 1280, 512
HALF = 192
LAST = 3
VMEM_BYTES = 62 << 20
N = 8
G = 48
W = 128


def kernel(v_hbm, t_hbm, out, v, t, p, sib, held, s1, r1, s2,
           load_sem, xs_sem, xr_sem, cs_sem, cr_sem, s1s_sem, s1r_sem, s2s_sem, s2r_sem):
    x, ij, z = lax.axis_index("ab"), lax.axis_index("ij"), lax.axis_index("cd")
    y, c = ij // 2, ij % 2
    xv, xt = x + 1 - 2 * (x % 2), 3 - x

    def at(xx, ii, zz):
        return {"ab": xx, "ij": ii, "cd": zz}

    twin = at(x, ij + 1 - 2 * c, z)

    def block(q):
        s = q // 4
        return 2 * (q % 4) + c + s * (1 - 2 * c)

    def over_z(q):
        return 1 if q == LAST else 1 - c

    def peer(zf, i):
        return at(x, 2 * (y + (1 - zf) * (i - y)) + c, z + zf * (i - z))

    def owner(q, zf):
        s, j = q // 4, block(q)
        me1 = y + zf * (z - y)
        return x + s * (xv - x), 4 * (x + (j // 4) * (xt - x)) + j % 4, me1

    def is_me(place):
        return (place[0] == x) & (place[1] == ij) & (place[2] == z)

    slab = ij // 4
    src_s = jnp.where((slab == x) | (slab == 3 - x), 0, 1)
    src_x = x + src_s * (xv - x)
    src_j = jnp.where(slab == src_x, 0, 4) + ij % 4
    src_c = (src_s + src_j) % 2
    src_q = 4 * src_s + src_j // 2
    src_zf = jnp.where((src_c == 0) | (src_q == LAST), 1, 0)

    def source(i):
        return src_x, 2 * (z + src_zf * (i - z)) + src_c, i + src_zf * (z - i)

    barrier = pltpu.get_barrier_semaphore()

    def greet(device):
        pl.semaphore_signal(barrier, inc=1, device_id=device, device_id_type=MESH)

    def greet_other(place):
        @pl.when(jnp.logical_not(is_me(place)))
        def _():
            greet(at(*place))

    greet(at(xt, ij, z))
    greet(at(xv, ij, z))
    greet(twin)

    loads = [pltpu.make_async_copy(v_hbm.at[:, h], v.at[0, h], load_sem.at[h]) for h in range(2)]
    loads.append(pltpu.make_async_copy(t_hbm, t.at[:, pl.ds(0, COLS)], load_sem.at[2]))
    for load in loads:
        load.start()

    for d in range(1, N):
        greet(peer(1, (z + d) % N))

    @pl.when(c == 1)
    def _():
        for d in range(1, N):
            greet(peer(0, (y + d) % N))

    for q in range(N):
        greet_other(owner(q, over_z(q)))
    for i in range(N):
        greet_other(source(i))

    mine = jnp.where(is_me(source(y + (1 - src_zf) * (z - y))), 1, 0)

    def settle(count):
        pl.semaphore_wait(barrier, count)

    for cc in range(2):
        for m in range(2):
            @pl.when((c == cc) & (mine == m))
            def _():
                settle(3 + 7 + 7 * cc + 16 - 2 * m)

    swaps = []
    for i in range(4):
        swaps.append(pltpu.make_async_remote_copy(
            src_ref=t_hbm.at[:, pl.ds(i * W, W)], dst_ref=t.at[:, pl.ds(COLS + i * W, W)],
            send_sem=xs_sem.at[i], recv_sem=xr_sem.at[i], device_id=at(xt, ij, z), device_id_type=MESH))
    for h in range(2):
        swaps.append(pltpu.make_async_remote_copy(
            src_ref=v_hbm.at[:, h], dst_ref=v.at[1, h], send_sem=xs_sem.at[4 + h], recv_sem=xr_sem.at[4 + h],
            device_id=at(xv, ij, z), device_id_type=MESH))
    for i in (0, 4, 1, 5, 2, 3):
        swaps[i].start()

    def to_twin(q, h):
        mine_b = block(q) % 2
        pltpu.make_async_remote_copy(
            src_ref=p.at[q, 1 - mine_b, h], dst_ref=sib.at[q, h], send_sem=cs_sem, recv_sem=cr_sem.at[q, h],
            device_id=twin, device_id_type=MESH).start()

    def pair(q, h):
        rows = v[q // 4, h].reshape(HALF, DEPTH)
        res = jnp.dot(rows, t[:, pl.ds(256 * (q % 4), 256)], preferred_element_type=F32)
        p[q, 0, h] = res[:, :W]
        p[q, 1, h] = res[:, W:]
        to_twin(q, h)

    def single(s, h, j):
        q = 4 * s + j // 2
        rows = v[s, h].reshape(HALF, DEPTH)
        p[q, j % 2, h] = jnp.dot(rows, t[:, pl.ds(W * j, W)], preferred_element_type=F32)

        @pl.when(c != (s + j) % 2)
        def _():
            to_twin(q, h)

    def scatter(q, h, zf):
        pltpu.make_async_copy(sib.at[q, h], sib.at[q, h], cr_sem.at[q, h]).wait()
        held[q, h] = p[q, block(q) % 2, h] + sib[q, h]
        me1 = y + zf * (z - y)
        for i in range(4):
            g = 2 * i + h

            @pl.when(g != me1)
            def _():
                pltpu.make_async_remote_copy(
                    src_ref=held.at[q, h, pl.ds(G * i, G)], dst_ref=s1.at[q, (g - me1 + N) % N],
                    send_sem=s1s_sem, recv_sem=s1r_sem.at[q], device_id=peer(zf, g), device_id_type=MESH).start()

    def gather(q, zf):
        pltpu.make_async_copy(s1.at[q, pl.ds(1, N - 1)], s1.at[q, pl.ds(1, N - 1)], s1r_sem.at[q]).wait()
        me1 = y + zf * (z - y)
        me2 = z + zf * (y - z)
        total = held[q, me1 % 2, pl.ds(pl.multiple_of(me1 // 2 * G, G), G), :]
        for d in range(1, N):
            total = total + s1[q, d]
        place = owner(q, zf)
        here = is_me(place)

        @pl.when(here)
        def _():
            s2[me2] = total
            r1[q] = total

        @pl.when(jnp.logical_not(here))
        def _():
            r1[q] = total
            pltpu.make_async_remote_copy(
                src_ref=r1.at[q], dst_ref=s2.at[me2], send_sem=s2s_sem, recv_sem=s2r_sem,
                device_id=at(*place), device_id_type=MESH).start()

    for load in loads:
        load.wait()
    for q in (0, 1):
        for h in (0, 1):
            pair(q, h)
    for q in (0, 1):
        for h in (0, 1):
            scatter(q, h, 1 - c)
    swaps[0].wait_recv()
    single(0, 0, 4)
    single(0, 1, 4)
    swaps[4].wait_recv()
    pair(4, 0)
    pair(5, 0)
    single(1, 0, 4)
    gather(0, 1 - c)
    gather(1, 1 - c)
    scatter(4, 0, 1 - c)
    scatter(5, 0, 1 - c)
    swaps[1].wait_recv()
    single(0, 0, 5)
    single(0, 1, 5)
    single(1, 0, 5)
    scatter(2, 0, 1 - c)
    scatter(2, 1, 1 - c)
    scatter(6, 0, 1 - c)
    swaps[5].wait_recv()
    pair(4, 1)
    pair(5, 1)
    single(1, 1, 4)
    single(1, 1, 5)
    scatter(4, 1, 1 - c)
    scatter(5, 1, 1 - c)
    scatter(6, 1, 1 - c)
    swaps[2].wait_recv()
    single(0, 0, 6)
    single(0, 1, 6)
    single(1, 0, 6)
    single(1, 1, 6)
    for cc in range(2):
        @pl.when(c == cc)
        def _():
            scatter(3 + 4 * cc, 0, 1 - cc)
            scatter(3 + 4 * cc, 1, 1 - cc)
    gather(2, 1 - c)
    swaps[3].wait_recv()
    single(0, 0, 7)
    single(0, 1, 7)
    single(1, 0, 7)
    single(1, 1, 7)
    for cc in range(2):
        @pl.when(c == cc)
        def _():
            scatter(7 - 4 * cc, 0, 1)
            scatter(7 - 4 * cc, 1, 1)
    gather(4, 1 - c)
    gather(5, 1 - c)
    gather(6, 1 - c)
    for cc in range(2):
        @pl.when(c == cc)
        def _():
            gather(3 + 4 * cc, 1 - cc)
            gather(7 - 4 * cc, 1)

    for m in range(2):
        @pl.when(mine == m)
        def _():
            pltpu.make_async_copy(s2.at[pl.ds(0, N - m)], s2.at[pl.ds(0, N - m)], s2r_sem).wait()
    total = s2[0]
    for d in range(1, N):
        total = total + s2[d]
    out[...] = total.astype(BF16)

    for swap in swaps:
        swap.wait_send()
    pltpu.make_async_copy(sib, sib, cs_sem).wait()
    pltpu.make_async_copy(s1.at[:, pl.ds(1, N - 1)], s1.at[:, pl.ds(1, N - 1)], s1s_sem).wait()
    for m in range(2):
        @pl.when(mine == m)
        def _():
            pltpu.make_async_copy(s2.at[pl.ds(0, N - m)], s2.at[pl.ds(0, N - m)], s2s_sem).wait()


def per_device(integrals, amplitudes):
    dma, vmem = pltpu.SemaphoreType.DMA, pltpu.VMEM
    return pl.pallas_call(
        kernel,
        out_shape=jax.ShapeDtypeStruct((G, W), BF16),
        in_specs=[pl.BlockSpec(memory_space=pl.ANY)] * 2,
        out_specs=pl.BlockSpec(memory_space=pltpu.VMEM),
        scratch_shapes=[
            vmem((2, 2, 4, G, DEPTH), BF16),
            vmem((DEPTH, 2 * COLS), BF16),
            vmem((N, 2, 2, HALF, W), F32),
            vmem((N, 2, HALF, W), F32),
            vmem((N, 2, HALF, W), F32),
            vmem((N, N, G, W), F32),
            vmem((N, G, W), F32),
            vmem((N, G, W), F32),
            dma((3,)), dma((6,)), dma((6,)),
            dma, dma((N, 2)), dma, dma((N,)), dma, dma,
        ],
        compiler_params=pltpu.CompilerParams(
            collective_id=0, has_side_effects=True, vmem_limit_bytes=VMEM_BYTES
        ),
    )(integrals.reshape(4, 2, G, DEPTH), amplitudes)


def solution(mesh):
    placed = (P("ab", ("cd", "ij")), P(("cd", "ij"), "ab"))
    return jax.shard_map(
        per_device, mesh=mesh, in_specs=placed, out_specs=P(("ab", "cd"), "ij"), check_vma=False
    )
```

```python
import jax
import jax.numpy as jnp
from jax import lax
from jax.experimental import pallas as pl
from jax.experimental.pallas import tpu as pltpu
from jax.sharding import PartitionSpec as P

MESH = pl.DeviceIdType.MESH
F32 = jnp.float32
BF16 = jnp.bfloat16
ROWS, DEPTH, COLS = 384, 1280, 512
HALF = 192
VMEM_BYTES = 62 << 20
N = 8
G = 48
W = 128


def kernel(v_hbm, t_hbm, out, v, t, p, sib, held, s1, r1, s2,
           load_sem, xs_sem, xr_sem, cs_sem, cr_sem, s1s_sem, s1r_sem, s2s_sem, s2r_sem, line_sem, wide_sem):
    x, ij, z = lax.axis_index("ab"), lax.axis_index("ij"), lax.axis_index("cd")
    y, c = ij // 2, ij % 2
    xv, xt = x + 1 - 2 * (x % 2), 3 - x

    def at(xx, ii, zz):
        return {"ab": xx, "ij": ii, "cd": zz}

    twin = at(x, ij + 1 - 2 * c, z)

    me1 = z + c * (y - z)
    me2 = y + c * (z - y)

    def block(q):
        s = q // 4
        return 2 * (q % 4) + c + s * (1 - 2 * c)

    def peer(i):
        return at(x, 2 * (y + c * (i - y)) + c, z + (1 - c) * (i - z))

    def owner(q):
        s, j = q // 4, block(q)
        return x + s * (xv - x), 4 * (x + (j // 4) * (xt - x)) + j % 4, me1

    def is_me(place):
        return (place[0] == x) & (place[1] == ij) & (place[2] == z)

    slab = ij // 4
    own_s = (slab == x) | (slab == 3 - x)
    mine = jnp.where(own_s & ((c == 0) | (y == z)), 1, 0)

    barrier = pltpu.get_barrier_semaphore()

    def signal(sem, device):
        pl.semaphore_signal(sem, inc=1, device_id=device, device_id_type=MESH)

    signal(barrier, at(xt, 2 * y, z))
    signal(barrier, at(xv, 2 * y, z))

    loads = [pltpu.make_async_copy(v_hbm.at[:, h], v.at[0, h], load_sem.at[h]) for h in range(2)]
    loads.append(pltpu.make_async_copy(t_hbm, t.at[:, pl.ds(0, COLS)], load_sem.at[2]))

    @pl.when(c == 0)
    def _():
        pl.semaphore_wait(barrier, 5)
        signal(line_sem, twin)

    @pl.when(c == 1)
    def _():
        signal(barrier, twin)
        pl.semaphore_wait(line_sem, 1)

    swaps = []
    for i in range(4):
        swaps.append(pltpu.make_async_remote_copy(
            src_ref=t_hbm.at[:, pl.ds(i * W, W)], dst_ref=t.at[:, pl.ds(COLS + i * W, W)],
            send_sem=xs_sem.at[i], recv_sem=xr_sem.at[i], device_id=at(xt, ij, z), device_id_type=MESH))
    for h in range(2):
        swaps.append(pltpu.make_async_remote_copy(
            src_ref=v_hbm.at[:, h], dst_ref=v.at[1, h], send_sem=xs_sem.at[4 + h], recv_sem=xr_sem.at[4 + h],
            device_id=at(xv, ij, z), device_id_type=MESH))
    for i in (0, 4, 1, 5, 2, 3):
        swaps[i].start()

    for load in loads:
        load.start()

    @pl.when(c == 1)
    def _():
        for d in range(1, N):
            signal(barrier, at(x, ij, (z + d) % N))
            signal(barrier, at(x, 2 * ((y + d) % N) + 1, z))

    def to_twin(q, h):
        mine_b = block(q) % 2
        pltpu.make_async_remote_copy(
            src_ref=p.at[q, 1 - mine_b, h], dst_ref=sib.at[q, h], send_sem=cs_sem, recv_sem=cr_sem.at[q, h],
            device_id=twin, device_id_type=MESH).start()

    def pair(q, h):
        rows = v[q // 4, h].reshape(HALF, DEPTH)
        res = jnp.dot(rows, t[:, pl.ds(256 * (q % 4), 256)], preferred_element_type=F32)
        p[q, 0, h] = res[:, :W]
        p[q, 1, h] = res[:, W:]
        to_twin(q, h)

    def single(s, h, j):
        q = 4 * s + j // 2
        rows = v[s, h].reshape(HALF, DEPTH)
        p[q, j % 2, h] = jnp.dot(rows, t[:, pl.ds(W * j, W)], preferred_element_type=F32)

        @pl.when(c != (s + j) % 2)
        def _():
            to_twin(q, h)

    def scatter(q, h):
        pltpu.make_async_copy(sib.at[q, h], sib.at[q, h], cr_sem.at[q, h]).wait()
        held[q, h] = p[q, block(q) % 2, h] + sib[q, h]
        for i in range(4):
            g = 2 * i + h

            @pl.when(g != me1)
            def _():
                pltpu.make_async_remote_copy(
                    src_ref=held.at[q, h, pl.ds(G * i, G)], dst_ref=s1.at[q, (g - me1 + N) % N],
                    send_sem=s1s_sem, recv_sem=s1r_sem.at[q], device_id=peer(g), device_id_type=MESH).start()

    def gather(q):
        pltpu.make_async_copy(s1.at[q, pl.ds(1, N - 1)], s1.at[q, pl.ds(1, N - 1)], s1r_sem.at[q]).wait()
        total = held[q, me1 % 2, pl.ds(pl.multiple_of(me1 // 2 * G, G), G), :]
        for d in range(1, N):
            total = total + s1[q, d]
        place = owner(q)
        here = is_me(place)

        @pl.when(here)
        def _():
            s2[me2] = total
            r1[q] = total

        @pl.when(jnp.logical_not(here))
        def _():
            r1[q] = total
            pltpu.make_async_remote_copy(
                src_ref=r1.at[q], dst_ref=s2.at[me2], send_sem=s2s_sem, recv_sem=s2r_sem,
                device_id=at(*place), device_id_type=MESH).start()

    for load in loads:
        load.wait()
    for q in (0, 1):
        for h in (0, 1):
            pair(q, h)

    @pl.when(c == 1)
    def _():
        pl.semaphore_wait(barrier, 2 * (N - 1))
        signal(wide_sem, twin)

    @pl.when(c == 0)
    def _():
        pl.semaphore_wait(wide_sem, 1)

    for q in (0, 1):
        for h in (0, 1):
            scatter(q, h)
    swaps[0].wait_recv()
    single(0, 0, 4)
    single(0, 1, 4)
    swaps[4].wait_recv()
    pair(4, 0)
    pair(5, 0)
    single(1, 0, 4)
    gather(0)
    gather(1)
    scatter(4, 0)
    scatter(5, 0)
    swaps[1].wait_recv()
    single(0, 0, 5)
    single(0, 1, 5)
    single(1, 0, 5)
    scatter(2, 0)
    scatter(2, 1)
    scatter(6, 0)
    swaps[5].wait_recv()
    pair(4, 1)
    pair(5, 1)
    single(1, 1, 4)
    single(1, 1, 5)
    scatter(4, 1)
    scatter(5, 1)
    scatter(6, 1)
    swaps[2].wait_recv()
    single(0, 0, 6)
    single(0, 1, 6)
    single(1, 0, 6)
    single(1, 1, 6)
    for cc in range(2):
        @pl.when(c == cc)
        def _():
            scatter(3 + 4 * cc, 0)
            scatter(3 + 4 * cc, 1)
    gather(2)
    swaps[3].wait_recv()
    single(0, 0, 7)
    single(0, 1, 7)
    single(1, 0, 7)
    single(1, 1, 7)
    for cc in range(2):
        @pl.when(c == cc)
        def _():
            scatter(7 - 4 * cc, 0)
            scatter(7 - 4 * cc, 1)
    gather(4)
    gather(5)
    gather(6)
    for cc in range(2):
        @pl.when(c == cc)
        def _():
            gather(3 + 4 * cc)
            gather(7 - 4 * cc)

    for m in range(2):
        @pl.when(mine == m)
        def _():
            pltpu.make_async_copy(s2.at[pl.ds(0, N - m)], s2.at[pl.ds(0, N - m)], s2r_sem).wait()
    total = s2[0]
    for d in range(1, N):
        total = total + s2[d]
    out[...] = total.astype(BF16)

    for swap in swaps:
        swap.wait_send()
    pltpu.make_async_copy(sib, sib, cs_sem).wait()
    pltpu.make_async_copy(s1.at[:, pl.ds(1, N - 1)], s1.at[:, pl.ds(1, N - 1)], s1s_sem).wait()
    for m in range(2):
        @pl.when(mine == m)
        def _():
            pltpu.make_async_copy(s2.at[pl.ds(0, N - m)], s2.at[pl.ds(0, N - m)], s2s_sem).wait()


def per_device(integrals, amplitudes):
    dma, vmem = pltpu.SemaphoreType.DMA, pltpu.VMEM
    return pl.pallas_call(
        kernel,
        out_shape=jax.ShapeDtypeStruct((G, W), BF16),
        in_specs=[pl.BlockSpec(memory_space=pl.ANY)] * 2,
        out_specs=pl.BlockSpec(memory_space=pltpu.VMEM),
        scratch_shapes=[
            vmem((2, 2, 4, G, DEPTH), BF16),
            vmem((DEPTH, 2 * COLS), BF16),
            vmem((N, 2, 2, HALF, W), F32),
            vmem((N, 2, HALF, W), F32),
            vmem((N, 2, HALF, W), F32),
            vmem((N, N, G, W), F32),
            vmem((N, G, W), F32),
            vmem((N, G, W), F32),
            dma((3,)), dma((6,)), dma((6,)),
            dma, dma((N, 2)), dma, dma((N,)), dma, dma,
            pltpu.SemaphoreType.REGULAR, pltpu.SemaphoreType.REGULAR,
        ],
        compiler_params=pltpu.CompilerParams(
            collective_id=0, has_side_effects=True, vmem_limit_bytes=VMEM_BYTES
        ),
    )(integrals.reshape(4, 2, G, DEPTH), amplitudes)


def solution(mesh):
    placed = (P("ab", ("cd", "ij")), P(("cd", "ij"), "ab"))
    return jax.shard_map(
        per_device, mesh=mesh, in_specs=placed, out_specs=P(("ab", "cd"), "ij"), check_vma=False
    )
```

```python
import jax
import jax.numpy as jnp
from jax import lax
from jax.experimental import pallas as pl
from jax.experimental.pallas import tpu as pltpu
from jax.sharding import PartitionSpec as P

MESH = pl.DeviceIdType.MESH
F32 = jnp.float32
BF16 = jnp.bfloat16
ROWS, DEPTH, COLS = 384, 1280, 512
PART = 96
VMEM_BYTES = 53 << 20
N = 8
G = 48
W = 128
Z_FIRST = (5,)
ALL = (0, 4)


def kernel(v_hbm, t_hbm, out, v, t, p, sib, held, s1, r1, s2,
           load_sem, xs_sem, xr_sem, cs_sem, cr_sem, s1s_sem, s1r_sem, s2s_sem, s2r_sem, line_sem, wide_sem):
    x, ij, z = lax.axis_index("ab"), lax.axis_index("ij"), lax.axis_index("cd")
    y, c = ij // 2, ij % 2
    xv, xt = x + 1 - 2 * (x % 2), 3 - x

    def at(xx, ii, zz):
        return {"ab": xx, "ij": ii, "cd": zz}

    twin = at(x, ij + 1 - 2 * c, z)

    def axes(q):
        yf = c * (0 if isinstance(q, int) and q in Z_FIRST else 1)
        return yf, z + yf * (y - z), y + yf * (z - y)

    def block(q):
        s = q // 4
        return 2 * (q % 4) + c + s * (1 - 2 * c)

    def peer(yf, i):
        return at(x, 2 * (y + yf * (i - y)) + c, z + (1 - yf) * (i - z))

    def owner(q):
        s, j = q // 4, block(q)
        return x + s * (xv - x), 4 * (x + (j // 4) * (xt - x)) + j % 4, axes(q)[1]

    def is_me(place):
        return (place[0] == x) & (place[1] == ij) & (place[2] == z)

    slab = ij // 4
    own_s = (slab == x) | (slab == 3 - x)
    mine = jnp.where(own_s & ((c == 0) | (y == z)), 1, 0)

    barrier = pltpu.get_barrier_semaphore()

    def signal(sem, device):
        pl.semaphore_signal(sem, inc=1, device_id=device, device_id_type=MESH)

    signal(barrier, at(xt, 2 * y, z))
    signal(barrier, at(xv, 2 * y, z))

    loads = [pltpu.make_async_copy(v_hbm.at[:, h], v.at[0, h], load_sem.at[h]) for h in range(4)]
    loads.append(pltpu.make_async_copy(t_hbm, t.at[:, pl.ds(0, COLS)], load_sem.at[4]))

    @pl.when(c == 0)
    def _():
        pl.semaphore_wait(barrier, 5)
        signal(line_sem, twin)

    @pl.when(c == 1)
    def _():
        signal(barrier, twin)
        pl.semaphore_wait(line_sem, 1)

    def remote(src, dst, send, recv, device):
        return pltpu.make_async_remote_copy(
            src_ref=src, dst_ref=dst, send_sem=send, recv_sem=recv, device_id=device, device_id_type=MESH)

    over_t, over_v = at(xt, ij, z), at(xv, ij, z)
    swaps = [remote(t_hbm.at[:, pl.ds(i * W, W)], t.at[:, pl.ds(COLS + i * W, W)], xs_sem.at[i], xr_sem.at[i], over_t)
             for i in range(4)]
    swaps += [remote(v_hbm.at[:, h], v.at[1, h], xs_sem.at[4 + h], xr_sem.at[4 + h], over_v) for h in range(4)]
    for i in (0, 4, 1, 5, 2, 6, 3, 7):
        swaps[i].start()

    for load in loads:
        load.start()

    @pl.when(c == 1)
    def _():
        for d in range(1, N):
            signal(barrier, at(x, ij, (z + d) % N))
            signal(barrier, at(x, 2 * ((y + d) % N) + 1, z))

    def to_twin(src, dst, sem):
        remote(src, dst, cs_sem, sem, twin).start()

    def pair(s, jj, parts):
        q = 4 * s + jj
        lo, n = parts
        rows = v[s, pl.ds(lo, n)].reshape(n * PART, DEPTH)
        res = jnp.dot(rows, t[:, pl.ds(2 * W * jj, 2 * W)], preferred_element_type=F32)
        for b in range(2):
            p[q, b, pl.ds(lo, n)] = res[:, b * W:(b + 1) * W].reshape(n, PART, W)
        other = 1 - block(q) % 2
        to_twin(p.at[q, other, pl.ds(lo, n)], sib.at[q, pl.ds(lo, n)], cr_sem.at[q, lo])

    def single(s, j, parts):
        q = 4 * s + j // 2
        lo, n = parts
        rows = v[s, pl.ds(lo, n)].reshape(n * PART, DEPTH)
        res = jnp.dot(rows, t[:, pl.ds(W * j, W)], preferred_element_type=F32)
        p[q, j % 2, pl.ds(lo, n)] = res.reshape(n, PART, W)

        @pl.when(c != (s + j) % 2)
        def _():
            to_twin(p.at[q, j % 2, pl.ds(lo, n)], sib.at[q, pl.ds(lo, n)], cr_sem.at[q, lo])

    def add_twin(q, parts):
        lo, n = parts
        piece = sib.at[q, pl.ds(lo, n)]
        pltpu.make_async_copy(piece, piece, cr_sem.at[q, lo]).wait()
        held[q, pl.ds(lo, n)] = p[q, block(q) % 2, pl.ds(lo, n)] + sib[q, pl.ds(lo, n)]

    def to_peer(q, h, i, slot):
        remote(held.at[q, h, pl.ds(pl.multiple_of(G * i, G), G)], s1.at[q, slot], s1s_sem, s1r_sem.at[q], peer(axes(q)[0], h + 4 * i)).start()

    def scatter(q):
        add_twin(q, ALL)
        me1 = axes(q)[1]
        for d in range(1, N):
            to = (me1 + d) % N
            to_peer(q, to % 4, to // 4, d)

    def scatter_part(q, h):
        add_twin(q, (h, 1))
        me1 = axes(q)[1]
        for i in range(2):
            g = h + 4 * i

            @pl.when(g != me1)
            def _():
                to_peer(q, h, i, (g - me1 + N) % N)

    def gather(q):
        pltpu.make_async_copy(s1.at[q, pl.ds(1, N - 1)], s1.at[q, pl.ds(1, N - 1)], s1r_sem.at[q]).wait()
        yf, me1, me2 = axes(q)
        total = held[q, me1 % 4, pl.ds(pl.multiple_of(me1 // 4 * G, G), G), :]
        for d in range(1, N):
            total = total + s1[q, d]
        place = owner(q)
        here = is_me(place)

        @pl.when(here)
        def _():
            s2[me2] = total
            r1[q] = total

        @pl.when(jnp.logical_not(here))
        def _():
            r1[q] = total
            pltpu.make_async_remote_copy(
                src_ref=r1.at[q], dst_ref=s2.at[me2], send_sem=s2s_sem, recv_sem=s2r_sem,
                device_id=at(*place), device_id_type=MESH).start()

    for load in loads:
        load.wait()
    pair(0, 0, ALL)
    pair(0, 1, ALL)

    @pl.when(c == 1)
    def _():
        pl.semaphore_wait(barrier, 2 * (N - 1))
        signal(wide_sem, twin)

    @pl.when(c == 0)
    def _():
        pl.semaphore_wait(wide_sem, 1)

    scatter(0)
    scatter(1)
    swaps[4].wait_recv()
    pair(1, 0, (0, 1))
    pair(1, 1, (0, 1))
    scatter_part(4, 0)
    scatter_part(5, 0)
    swaps[0].wait_recv()
    single(0, 4, ALL)
    swaps[5].wait_recv()
    pair(1, 0, (1, 1))
    pair(1, 1, (1, 1))
    single(1, 4, (0, 1))
    single(1, 4, (1, 1))
    scatter_part(4, 1)
    scatter_part(5, 1)
    swaps[1].wait_recv()
    single(0, 5, ALL)
    single(1, 5, (0, 1))
    single(1, 5, (1, 1))
    scatter(2)
    scatter_part(6, 0)
    scatter_part(6, 1)

    gather(0)
    gather(1)
    for h in (2, 3):
        swaps[4 + h].wait_recv()
        pair(1, 0, (h, 1))
        pair(1, 1, (h, 1))
        single(1, 4, (h, 1))
        single(1, 5, (h, 1))
        for q in (4, 5, 6):
            scatter_part(q, h)
    swaps[2].wait_recv()
    single(0, 6, ALL)
    single(1, 6, ALL)
    scatter(3 + 4 * c)
    gather(2)
    swaps[3].wait_recv()
    for cc in range(2):
        @pl.when(c == cc)
        def _():
            for lo in (0, 2):
                for s in (cc, 1 - cc):
                    single(s, 7, (lo, 2))

    def send_last(*groups):
        me1 = axes(7 - 4 * c)[1]
        for g in groups:
            @pl.when(g != me1)
            def _():
                to_peer(7 - 4 * c, g % 4, g // 4, (g - me1 + N) % N)

    add_twin(7 - 4 * c, (0, 2))
    send_last(0, 1)
    add_twin(7 - 4 * c, (2, 2))
    send_last(2, 3, 4, 5, 6, 7)
    gather(4)
    gather(5)
    gather(6)
    gather(3 + 4 * c)
    gather(7 - 4 * c)

    for m in range(2):
        @pl.when(mine == m)
        def _():
            pltpu.make_async_copy(s2.at[pl.ds(0, N - m)], s2.at[pl.ds(0, N - m)], s2r_sem).wait()
    total = s2[0]
    for d in range(1, N):
        total = total + s2[d]
    out[...] = total.astype(BF16)

    for swap in swaps:
        swap.wait_send()

    pltpu.make_async_copy(sib, sib, cs_sem).wait()
    pltpu.make_async_copy(s1.at[:, pl.ds(1, N - 1)], s1.at[:, pl.ds(1, N - 1)], s1s_sem).wait()
    for m in range(2):
        @pl.when(mine == m)
        def _():
            pltpu.make_async_copy(s2.at[pl.ds(0, N - m)], s2.at[pl.ds(0, N - m)], s2s_sem).wait()


def per_device(integrals, amplitudes):
    dma, vmem = pltpu.SemaphoreType.DMA, pltpu.VMEM
    return pl.pallas_call(
        kernel,
        out_shape=jax.ShapeDtypeStruct((G, W), BF16),
        in_specs=[pl.BlockSpec(memory_space=pl.ANY)] * 2,
        out_specs=pl.BlockSpec(memory_space=pltpu.VMEM),
        scratch_shapes=[
            vmem((2, 4, 2, G, DEPTH), BF16),
            vmem((DEPTH, 2 * COLS), BF16),
            vmem((N, 2, 4, PART, W), F32),
            vmem((N, 4, PART, W), F32),
            vmem((N, 4, PART, W), F32),
            vmem((N, N, G, W), F32),
            vmem((N, G, W), F32),
            vmem((N, G, W), F32),
            dma((5,)), dma((8,)), dma((8,)),
            dma, dma((N, 4)), dma, dma((N,)), dma, dma,
            pltpu.SemaphoreType.REGULAR, pltpu.SemaphoreType.REGULAR,
        ],
        compiler_params=pltpu.CompilerParams(
            collective_id=0, has_side_effects=True, vmem_limit_bytes=VMEM_BYTES
        ),
    )(integrals.reshape(2, 4, G, DEPTH), amplitudes)


def solution(mesh):
    placed = (P("ab", ("cd", "ij")), P(("cd", "ij"), "ab"))
    return jax.shard_map(
        per_device, mesh=mesh, in_specs=placed, out_specs=P(("ab", "cd"), "ij"), check_vma=False
    )
```

```python
import jax
import jax.numpy as jnp
from jax import lax
from jax.experimental import pallas as pl
from jax.experimental.pallas import tpu as pltpu
from jax.sharding import PartitionSpec as P

MESH = pl.DeviceIdType.MESH
F32 = jnp.float32
BF16 = jnp.bfloat16
ROWS, DEPTH, COLS = 384, 1280, 512
PART = 96
VMEM_BYTES = 53 << 20
N = 8
G = 48
W = 128
Z_FIRST = (5,)
ALL = (0, 4)


def kernel(v_hbm, t_hbm, out, v, t, p, sib, held, s1, r1, s2,
           load_sem, xs_sem, xr_sem, cs_sem, cr_sem, s1s_sem, s1r_sem, s2s_sem, s2r_sem, line_sem, wide_sem):
    x, ij, z = lax.axis_index("ab"), lax.axis_index("ij"), lax.axis_index("cd")
    y, c = ij // 2, ij % 2
    xv, xt = 3 - x, x + 1 - 2 * (x % 2)

    def at(xx, ii, zz):
        return {"ab": xx, "ij": ii, "cd": zz}

    twin = at(x, ij + 1 - 2 * c, z)

    def axes(q):
        yf = c * (0 if isinstance(q, int) and q in Z_FIRST else 1)
        return yf, z + yf * (y - z), y + yf * (z - y)

    def block(q):
        s = q // 4
        return 2 * (q % 4) + c + s * (1 - 2 * c)

    def peer(yf, i):
        return at(x, 2 * (y + yf * (i - y)) + c, z + (1 - yf) * (i - z))

    def owner(q):
        s, j = q // 4, block(q)
        return x + s * (xv - x), 4 * (x + (j // 4) * (xt - x)) + j % 4, axes(q)[1]

    def is_me(place):
        return (place[0] == x) & (place[1] == ij) & (place[2] == z)

    slab = ij // 4
    own_s = (slab == x) | (slab == xt)
    mine = jnp.where(own_s & ((c == 0) | (y == z)), 1, 0)

    barrier = pltpu.get_barrier_semaphore()

    def signal(sem, device):
        pl.semaphore_signal(sem, inc=1, device_id=device, device_id_type=MESH)

    signal(barrier, at(xt, 2 * y, z))
    signal(barrier, at(xv, 2 * y, z))

    loads = [pltpu.make_async_copy(v_hbm.at[:, h], v.at[0, h], load_sem.at[h]) for h in range(4)]
    loads.append(pltpu.make_async_copy(t_hbm, t.at[:, pl.ds(0, COLS)], load_sem.at[4]))
    for load in loads:
        load.start()

    @pl.when(c == 0)
    def _():
        pl.semaphore_wait(barrier, 5)
        signal(line_sem, twin)

    @pl.when(c == 1)
    def _():
        signal(barrier, twin)
        pl.semaphore_wait(line_sem, 1)

    def remote(src, dst, send, recv, device):
        return pltpu.make_async_remote_copy(
            src_ref=src, dst_ref=dst, send_sem=send, recv_sem=recv, device_id=device, device_id_type=MESH)

    over_t, over_v = at(xt, ij, z), at(xv, ij, z)
    swaps = [remote(t_hbm.at[:, pl.ds(i * W, W)], t.at[:, pl.ds(COLS + i * W, W)], xs_sem.at[i], xr_sem.at[i], over_t)
             for i in range(4)]
    swaps += [remote(v_hbm.at[:, h], v.at[1, h], xs_sem.at[4 + h], xr_sem.at[4 + h], over_v) for h in range(4)]
    for i in (0, 4, 1, 5, 2, 6, 3, 7):
        swaps[i].start()

    @pl.when(c == 1)
    def _():
        for d in range(1, N):
            signal(barrier, at(x, ij, (z + d) % N))
            signal(barrier, at(x, 2 * ((y + d) % N) + 1, z))

    def to_twin(src, dst, sem):
        remote(src, dst, cs_sem, sem, twin).start()

    def pair(s, jj, parts):
        q = 4 * s + jj
        lo, n = parts
        rows = v[s, pl.ds(lo, n)].reshape(n * PART, DEPTH)
        res = jnp.dot(rows, t[:, pl.ds(2 * W * jj, 2 * W)], preferred_element_type=F32)
        for b in range(2):
            p[q, b, pl.ds(lo, n)] = res[:, b * W:(b + 1) * W].reshape(n, PART, W)
        other = 1 - block(q) % 2
        to_twin(p.at[q, other, pl.ds(lo, n)], sib.at[q, pl.ds(lo, n)], cr_sem.at[q, lo])

    def single(s, j, parts):
        q = 4 * s + j // 2
        lo, n = parts
        rows = v[s, pl.ds(lo, n)].reshape(n * PART, DEPTH)
        res = jnp.dot(rows, t[:, pl.ds(W * j, W)], preferred_element_type=F32)
        p[q, j % 2, pl.ds(lo, n)] = res.reshape(n, PART, W)

        @pl.when(c != (s + j) % 2)
        def _():
            to_twin(p.at[q, j % 2, pl.ds(lo, n)], sib.at[q, pl.ds(lo, n)], cr_sem.at[q, lo])

    def add_twin(q, parts):
        lo, n = parts
        piece = sib.at[q, pl.ds(lo, n)]
        pltpu.make_async_copy(piece, piece, cr_sem.at[q, lo]).wait()
        held[q, pl.ds(lo, n)] = p[q, block(q) % 2, pl.ds(lo, n)] + sib[q, pl.ds(lo, n)]

    def to_peer(q, h, i, slot):
        remote(held.at[q, h, pl.ds(pl.multiple_of(G * i, G), G)], s1.at[q, slot], s1s_sem, s1r_sem.at[q], peer(axes(q)[0], h + 4 * i)).start()

    def scatter(q):
        add_twin(q, ALL)
        me1 = axes(q)[1]
        for d in range(1, N):
            to = (me1 + d) % N
            to_peer(q, to % 4, to // 4, d)

    def scatter_part(q, h):
        add_twin(q, (h, 1))
        me1 = axes(q)[1]
        for i in range(2):
            g = h + 4 * i

            @pl.when(g != me1)
            def _():
                to_peer(q, h, i, (g - me1 + N) % N)

    def gather(q):
        pltpu.make_async_copy(s1.at[q, pl.ds(1, N - 1)], s1.at[q, pl.ds(1, N - 1)], s1r_sem.at[q]).wait()
        yf, me1, me2 = axes(q)
        total = held[q, me1 % 4, pl.ds(pl.multiple_of(me1 // 4 * G, G), G), :]
        for d in range(1, N):
            total = total + s1[q, d]
        place = owner(q)
        here = is_me(place)

        @pl.when(here)
        def _():
            s2[me2] = total
            r1[q] = total

        @pl.when(jnp.logical_not(here))
        def _():
            r1[q] = total
            pltpu.make_async_remote_copy(
                src_ref=r1.at[q], dst_ref=s2.at[me2], send_sem=s2s_sem, recv_sem=s2r_sem,
                device_id=at(*place), device_id_type=MESH).start()

    for load in loads:
        load.wait()
    pair(0, 0, ALL)
    pair(0, 1, ALL)

    @pl.when(c == 1)
    def _():
        pl.semaphore_wait(barrier, 2 * (N - 1))
        signal(wide_sem, twin)

    @pl.when(c == 0)
    def _():
        pl.semaphore_wait(wide_sem, 1)

    scatter(0)
    scatter(1)
    swaps[4].wait_recv()
    pair(1, 0, (0, 1))
    pair(1, 1, (0, 1))
    scatter_part(4, 0)
    scatter_part(5, 0)
    swaps[0].wait_recv()
    single(0, 4, ALL)
    swaps[5].wait_recv()
    pair(1, 0, (1, 1))
    pair(1, 1, (1, 1))
    single(1, 4, (0, 1))
    single(1, 4, (1, 1))
    scatter_part(4, 1)
    scatter_part(5, 1)
    swaps[1].wait_recv()
    single(0, 5, ALL)
    single(1, 5, (0, 1))
    single(1, 5, (1, 1))
    scatter(2)
    scatter_part(6, 0)
    scatter_part(6, 1)

    gather(0)
    gather(1)
    for h in (2, 3):
        swaps[4 + h].wait_recv()
        pair(1, 0, (h, 1))
        pair(1, 1, (h, 1))
        single(1, 4, (h, 1))
        single(1, 5, (h, 1))
        for q in (4, 5, 6):
            scatter_part(q, h)
    swaps[2].wait_recv()
    single(0, 6, ALL)
    single(1, 6, ALL)
    scatter(3 + 4 * c)
    gather(2)
    swaps[3].wait_recv()
    for cc in range(2):
        @pl.when(c == cc)
        def _():
            for lo in (0, 2):
                for s in (cc, 1 - cc):
                    single(s, 7, (lo, 2))

    def send_last(*groups):
        me1 = axes(7 - 4 * c)[1]
        for g in groups:
            @pl.when(g != me1)
            def _():
                to_peer(7 - 4 * c, g % 4, g // 4, (g - me1 + N) % N)

    add_twin(7 - 4 * c, (0, 2))
    send_last(0, 1)
    add_twin(7 - 4 * c, (2, 2))
    send_last(2, 3, 4, 5, 6, 7)
    gather(4)
    gather(5)
    gather(6)
    gather(3 + 4 * c)
    gather(7 - 4 * c)

    for m in range(2):
        @pl.when(mine == m)
        def _():
            pltpu.make_async_copy(s2.at[pl.ds(0, N - m)], s2.at[pl.ds(0, N - m)], s2r_sem).wait()
    total = s2[0]
    for d in range(1, N):
        total = total + s2[d]
    out[...] = total.astype(BF16)

    for swap in swaps:
        swap.wait_send()

    pltpu.make_async_copy(sib, sib, cs_sem).wait()
    pltpu.make_async_copy(s1.at[:, pl.ds(1, N - 1)], s1.at[:, pl.ds(1, N - 1)], s1s_sem).wait()
    for m in range(2):
        @pl.when(mine == m)
        def _():
            pltpu.make_async_copy(s2.at[pl.ds(0, N - m)], s2.at[pl.ds(0, N - m)], s2s_sem).wait()


def per_device(integrals, amplitudes):
    dma, vmem = pltpu.SemaphoreType.DMA, pltpu.VMEM
    return pl.pallas_call(
        kernel,
        out_shape=jax.ShapeDtypeStruct((G, W), BF16),
        in_specs=[pl.BlockSpec(memory_space=pl.ANY)] * 2,
        out_specs=pl.BlockSpec(memory_space=pltpu.VMEM),
        scratch_shapes=[
            vmem((2, 4, 2, G, DEPTH), BF16),
            vmem((DEPTH, 2 * COLS), BF16),
            vmem((N, 2, 4, PART, W), F32),
            vmem((N, 4, PART, W), F32),
            vmem((N, 4, PART, W), F32),
            vmem((N, N, G, W), F32),
            vmem((N, G, W), F32),
            vmem((N, G, W), F32),
            dma((5,)), dma((8,)), dma((8,)),
            dma, dma((N, 4)), dma, dma((N,)), dma, dma,
            pltpu.SemaphoreType.REGULAR, pltpu.SemaphoreType.REGULAR,
        ],
        compiler_params=pltpu.CompilerParams(
            collective_id=0, has_side_effects=True, vmem_limit_bytes=VMEM_BYTES
        ),
    )(integrals.reshape(2, 4, G, DEPTH), amplitudes)


def solution(mesh):
    placed = (P("ab", ("cd", "ij")), P(("cd", "ij"), "ab"))
    return jax.shard_map(
        per_device, mesh=mesh, in_specs=placed, out_specs=P(("ab", "cd"), "ij"), check_vma=False
    )
```

```python
import jax
import jax.numpy as jnp
from jax import lax
from jax.experimental import pallas as pl
from jax.experimental.pallas import tpu as pltpu
from jax.sharding import PartitionSpec as P

MESH = pl.DeviceIdType.MESH
F32 = jnp.float32
BF16 = jnp.bfloat16
ROWS, DEPTH, COLS = 384, 1280, 512
PART = 96
VMEM_BYTES = 53 << 20
N = 8
G = 48
W = 128
Z_FIRST = (5,)
ALL = (0, 4)


def kernel(v_hbm, t_hbm, out, v, t, p, sib, held, s1, r1, s2,
           load_sem, xs_sem, xr_sem, cs_sem, cr_sem, s1s_sem, s1r_sem, s2s_sem, s2r_sem, line_sem, wide_sem):
    x, ij, z = lax.axis_index("ab"), lax.axis_index("ij"), lax.axis_index("cd")
    y, c = ij // 2, ij % 2
    xv, xt = 3 - x, x + 1 - 2 * (x % 2)

    def at(xx, ii, zz):
        return {"ab": xx, "ij": ii, "cd": zz}

    twin = at(x, ij + 1 - 2 * c, z)

    def axes(q):
        yf = c * (0 if isinstance(q, int) and q in Z_FIRST else 1)
        return yf, z + yf * (y - z), y + yf * (z - y)

    def block(q):
        s = q // 4
        return 2 * (q % 4) + c + s * (1 - 2 * c)

    def peer(yf, i):
        return at(x, 2 * (y + yf * (i - y)) + c, z + (1 - yf) * (i - z))

    def owner(q):
        s, j = q // 4, block(q)
        return x + s * (xv - x), 4 * (x + (j // 4) * (xt - x)) + j % 4, axes(q)[1]

    def is_me(place):
        return (place[0] == x) & (place[1] == ij) & (place[2] == z)

    slab = ij // 4
    own_s = (slab == x) | (slab == xt)
    mine = jnp.where(own_s & ((c == 0) | (y == z)), 1, 0)

    barrier = pltpu.get_barrier_semaphore()

    def signal(sem, device):
        pl.semaphore_signal(sem, inc=1, device_id=device, device_id_type=MESH)

    signal(barrier, at(xt, 2 * y, z))
    signal(barrier, at(xv, 2 * y, z))

    loads = [pltpu.make_async_copy(v_hbm.at[:, h], v.at[0, h], load_sem.at[h]) for h in range(4)]
    loads.append(pltpu.make_async_copy(t_hbm, t.at[:, pl.ds(0, COLS)], load_sem.at[4]))
    for load in loads:
        load.start()

    @pl.when(c == 0)
    def _():
        pl.semaphore_wait(barrier, 5)
        signal(line_sem, twin)

    @pl.when(c == 1)
    def _():
        signal(barrier, twin)
        pl.semaphore_wait(line_sem, 1)

    def remote(src, dst, send, recv, device):
        return pltpu.make_async_remote_copy(
            src_ref=src, dst_ref=dst, send_sem=send, recv_sem=recv, device_id=device, device_id_type=MESH)

    over_t, over_v = at(xt, ij, z), at(xv, ij, z)
    swaps = [remote(t_hbm.at[:, pl.ds(i * W, W)], t.at[:, pl.ds(COLS + i * W, W)], xs_sem.at[i], xr_sem.at[i], over_t)
             for i in range(4)]
    swaps += [remote(v_hbm.at[:, h], v.at[1, h], xs_sem.at[4 + h], xr_sem.at[4 + h], over_v) for h in range(4)]
    for i in (0, 4, 1, 5, 2, 6, 3, 7):
        swaps[i].start()

    @pl.when(c == 1)
    def _():
        for d in range(1, N):
            signal(barrier, at(x, ij, (z + d) % N))
            signal(barrier, at(x, 2 * ((y + d) % N) + 1, z))

    def to_twin(src, dst, sem):
        remote(src, dst, cs_sem, sem, twin).start()

    def pair(s, jj, parts):
        q = 4 * s + jj
        lo, n = parts
        rows = v[s, pl.ds(lo, n)].reshape(n * PART, DEPTH)
        res = jnp.dot(rows, t[:, pl.ds(2 * W * jj, 2 * W)], preferred_element_type=F32)
        for b in range(2):
            p[q, b, pl.ds(lo, n)] = res[:, b * W:(b + 1) * W].reshape(n, PART, W)
        other = 1 - block(q) % 2
        to_twin(p.at[q, other, pl.ds(lo, n)], sib.at[q, pl.ds(lo, n)], cr_sem.at[q, lo])

    def single(s, j, parts):
        q = 4 * s + j // 2
        lo, n = parts
        rows = v[s, pl.ds(lo, n)].reshape(n * PART, DEPTH)
        res = jnp.dot(rows, t[:, pl.ds(W * j, W)], preferred_element_type=F32)
        p[q, j % 2, pl.ds(lo, n)] = res.reshape(n, PART, W)

        @pl.when(c != (s + j) % 2)
        def _():
            to_twin(p.at[q, j % 2, pl.ds(lo, n)], sib.at[q, pl.ds(lo, n)], cr_sem.at[q, lo])

    def add_twin(q, parts):
        lo, n = parts
        piece = sib.at[q, pl.ds(lo, n)]
        pltpu.make_async_copy(piece, piece, cr_sem.at[q, lo]).wait()
        held[q, pl.ds(lo, n)] = p[q, block(q) % 2, pl.ds(lo, n)] + sib[q, pl.ds(lo, n)]

    def to_peer(q, h, i, slot):
        remote(held.at[q, h, pl.ds(pl.multiple_of(G * i, G), G)], s1.at[q, slot], s1s_sem, s1r_sem.at[q], peer(axes(q)[0], h + 4 * i)).start()

    def scatter(q):
        add_twin(q, ALL)
        me1 = axes(q)[1]
        for d in range(1, N):
            to = (me1 + d) % N
            to_peer(q, to % 4, to // 4, d)

    def scatter_part(q, h):
        add_twin(q, (h, 1))
        me1 = axes(q)[1]
        for i in range(2):
            g = h + 4 * i

            @pl.when(g != me1)
            def _():
                to_peer(q, h, i, (g - me1 + N) % N)

    def gather(q):
        pltpu.make_async_copy(s1.at[q, pl.ds(1, N - 1)], s1.at[q, pl.ds(1, N - 1)], s1r_sem.at[q]).wait()
        yf, me1, me2 = axes(q)
        total = held[q, me1 % 4, pl.ds(pl.multiple_of(me1 // 4 * G, G), G), :]
        for d in range(1, N):
            total = total + s1[q, d]
        place = owner(q)
        here = is_me(place)

        @pl.when(here)
        def _():
            s2[me2] = total
            r1[q] = total

        @pl.when(jnp.logical_not(here))
        def _():
            r1[q] = total
            pltpu.make_async_remote_copy(
                src_ref=r1.at[q], dst_ref=s2.at[me2], send_sem=s2s_sem, recv_sem=s2r_sem,
                device_id=at(*place), device_id_type=MESH).start()

    for load in loads:
        load.wait()
    pair(0, 0, ALL)
    pair(0, 1, ALL)

    @pl.when(c == 1)
    def _():
        pl.semaphore_wait(barrier, 2 * (N - 1))
        signal(wide_sem, twin)

    @pl.when(c == 0)
    def _():
        pl.semaphore_wait(wide_sem, 1)

    scatter(0)
    scatter(1)
    swaps[4].wait_recv()
    pair(1, 0, (0, 1))
    pair(1, 1, (0, 1))
    scatter_part(4, 0)
    scatter_part(5, 0)
    swaps[0].wait_recv()
    single(0, 4, ALL)
    swaps[5].wait_recv()
    pair(1, 0, (1, 1))
    pair(1, 1, (1, 1))
    single(1, 4, (0, 1))
    single(1, 4, (1, 1))
    scatter_part(4, 1)
    scatter_part(5, 1)
    swaps[1].wait_recv()
    single(0, 5, ALL)
    single(1, 5, (0, 1))
    single(1, 5, (1, 1))
    scatter(2)
    scatter_part(6, 0)
    scatter_part(6, 1)

    gather(0)
    gather(1)
    for h in (2, 3):
        swaps[4 + h].wait_recv()
        pair(1, 0, (h, 1))
        pair(1, 1, (h, 1))
        single(1, 4, (h, 1))
        single(1, 5, (h, 1))
        for q in (4, 5, 6):
            scatter_part(q, h)
    swaps[2].wait_recv()
    single(0, 6, ALL)
    single(1, 6, ALL)
    scatter(3 + 4 * c)
    gather(2)
    swaps[3].wait_recv()
    for cc in range(2):
        @pl.when(c == cc)
        def _():
            for lo in (0, 2):
                for s in (cc, 1 - cc):
                    single(s, 7, (lo, 2))

    def send_last(*groups):
        me1 = axes(7 - 4 * c)[1]
        for g in groups:
            @pl.when(g != me1)
            def _():
                to_peer(7 - 4 * c, g % 4, g // 4, (g - me1 + N) % N)

    add_twin(7 - 4 * c, (0, 2))
    send_last(0, 1)
    add_twin(7 - 4 * c, (2, 2))
    send_last(3, 2, 4, 5, 6, 7)
    gather(4)
    gather(5)
    gather(6)
    gather(3 + 4 * c)
    gather(7 - 4 * c)

    for m in range(2):
        @pl.when(mine == m)
        def _():
            pltpu.make_async_copy(s2.at[pl.ds(0, N - m)], s2.at[pl.ds(0, N - m)], s2r_sem).wait()
    total = s2[0]
    for d in range(1, N):
        total = total + s2[d]
    out[...] = total.astype(BF16)

    for swap in swaps:
        swap.wait_send()

    pltpu.make_async_copy(sib, sib, cs_sem).wait()
    pltpu.make_async_copy(s1.at[:, pl.ds(1, N - 1)], s1.at[:, pl.ds(1, N - 1)], s1s_sem).wait()
    for m in range(2):
        @pl.when(mine == m)
        def _():
            pltpu.make_async_copy(s2.at[pl.ds(0, N - m)], s2.at[pl.ds(0, N - m)], s2s_sem).wait()


def per_device(integrals, amplitudes):
    dma, vmem = pltpu.SemaphoreType.DMA, pltpu.VMEM
    return pl.pallas_call(
        kernel,
        out_shape=jax.ShapeDtypeStruct((G, W), BF16),
        in_specs=[pl.BlockSpec(memory_space=pl.ANY)] * 2,
        out_specs=pl.BlockSpec(memory_space=pltpu.VMEM),
        scratch_shapes=[
            vmem((2, 4, 2, G, DEPTH), BF16),
            vmem((DEPTH, 2 * COLS), BF16),
            vmem((N, 2, 4, PART, W), F32),
            vmem((N, 4, PART, W), F32),
            vmem((N, 4, PART, W), F32),
            vmem((N, N, G, W), F32),
            vmem((N, G, W), F32),
            vmem((N, G, W), F32),
            dma((5,)), dma((8,)), dma((8,)),
            dma, dma((N, 4)), dma, dma((N,)), dma, dma,
            pltpu.SemaphoreType.REGULAR, pltpu.SemaphoreType.REGULAR,
        ],
        compiler_params=pltpu.CompilerParams(
            collective_id=0, has_side_effects=True, vmem_limit_bytes=VMEM_BYTES
        ),
    )(integrals.reshape(2, 4, G, DEPTH), amplitudes)


def solution(mesh):
    placed = (P("ab", ("cd", "ij")), P(("cd", "ij"), "ab"))
    return jax.shard_map(
        per_device, mesh=mesh, in_specs=placed, out_specs=P(("ab", "cd"), "ij"), check_vma=False
    )
```
